256 devices in a mesh: frame: 4 (over y_lo, core), space: 64 (over x, y_hi, z).
Axes of the slice: x: 4, y: 4 (y_hi: 2, y_lo: 2; y = y_hi * 2 + y_lo), z: 8, core: 2. Of those that a mesh axis runs over, the one named last changes fastest.
Arguments:
- frames_in: bfloat16 [8, 8192, 2048], P('frame', 'space'), may hold values from -6 to 6
- levels: int32 [8], P('frame'), may hold values from 1 to 899
- fresh: bfloat16 [8192, 2048], P('space'), may hold values from -6 to 6
- w_mod: bfloat16 [256, 4096], replicated, may hold values from -0.375 to 0.375
- w_qkv: bfloat16 [2048, 3072], P('space'), may hold values from -0.26516504 to 0.26516504
- q_gain: float32 [8], replicated, may hold values from 0.5 to 64
- w_out: bfloat16 [1024, 2048], P('space'), may hold values from -0.1875 to 0.1875
Outputs:
- frames_out: bfloat16 [8, 8192, 2048], P('frame', 'space')
The draws below stay inside these ranges and needn't reach their ends.
All inputs are finite; a program needn't handle non-finite values.
Results may differ from the reference program's by a relative error of at most 0.0075.
The reference program's roundings to bfloat16 on the way count: a program that leaves them out, or rounds other values in their place, can miss the bound.
Values may be sent and summed in bfloat16 or wider, within the bound.
No kernel may reach another device: no remote copies, remote signals or barrier semaphores. Data moves between devices by JAX's collectives and lax.ppermute only.
A program may use at most 128 MiB of HBM per device.

```python
import math
import jax
import jax.numpy as jnp
from jax import lax

D = 2048
HEADS = 8
HD = 128
FREQ = 256
LEVELS = 1000
FRAMES = 8
HALF = 128
TOKENS = 8192


def draw_frames_in(key, part):
    key = jax.random.fold_in(key, 11)
    first_key, second_key = jax.random.split(key)
    common = jax.random.normal(first_key, (TOKENS, D), jnp.float32)
    noise = jax.random.normal(second_key, (FRAMES, TOKENS, D), jnp.float32)
    values = common[None] + 0.5 * noise
    return jnp.clip(values, -6.0, 6.0).astype(jnp.bfloat16)


def draw_w_mod(key, part):
    key = jax.random.fold_in(key, 12)
    values = jax.random.normal(key, (FREQ, 2 * D), jnp.float32)
    values = jnp.clip(values, -6.0, 6.0) * FREQ ** (-0.5)
    return values.astype(jnp.bfloat16)


def draw_w_qkv(key, part):
    key = jax.random.fold_in(key, 13)
    first_key = jax.random.fold_in(key, 0)
    inner = HEADS * HD
    base = jnp.clip(jax.random.normal(first_key, (D, 3 * inner), jnp.float32), -3.0, 3.0)
    query_part = base[:, :inner]
    key_part = 0.5 * query_part + 0.866 * base[:, inner:2 * inner]
    values = jnp.concatenate([query_part, key_part, base[:, 2 * inner:]], axis=1) * D ** (-0.5)
    return values.astype(jnp.bfloat16)


def draw_q_gain(key, part):
    key = jax.random.fold_in(key, 17)
    second_key = jax.random.fold_in(key, 1)
    values = jnp.exp(jax.random.uniform(second_key, (HEADS,), jnp.float32, math.log(0.5), math.log(8.0)))
    return values.astype(jnp.float32)


def with_ends(result, key, smallest, largest):
    shape = result.shape
    index_at = [jax.random.randint(jax.random.fold_in(key, axis), (), 0, shape[axis]) for axis in range(len(shape))]
    result = result.at[tuple(index_at)].set(smallest)
    longest = shape.index(max(shape))
    index_at[longest] = (index_at[longest] + 1) % shape[longest]
    return result.at[tuple(index_at)].set(largest)


def block_scale(own_key, extent, cuts, smallest, high):
    loudness = 1.0
    for position, shards_of in cuts:
        steps = jax.random.uniform(jax.random.fold_in(jax.random.fold_in(own_key, 6), position), (shards_of,), jnp.float32, smallest / len(cuts), high / len(cuts))
        loudness = loudness * jnp.repeat(jnp.exp(steps), extent[position] // shards_of).reshape((-1,) + (1,) * (len(extent) - 1 - position))
    return loudness


def bell_draw(key, dims, scale, bound, cuts=(), held_as=jnp.bfloat16):
    loudness = block_scale(key, dims, cuts, -0.22, 0.18) if cuts else 1.0
    array = jax.random.normal(key, dims, jnp.float32) * scale * loudness
    return jnp.minimum(jnp.maximum(array, -bound), bound).astype(held_as)


def setup_inputs(seed: int = 0) -> dict:
    key_of = jax.random.split(jax.random.key(seed), 8)
    return {
        "frames_in": draw_frames_in(jax.random.fold_in(key_of[7], 71), 0),
        "levels": with_ends(jax.random.randint(key_of[1], (FRAMES,), 1, 900), jax.random.fold_in(key_of[1], 1), 1, 899).astype(jnp.int32),
        "fresh": bell_draw(key_of[2], (TOKENS, D), 1.0, 6.0, ((0, 64),)),
        "w_mod": draw_w_mod(jax.random.fold_in(key_of[7], 71), 0),
        "w_qkv": draw_w_qkv(jax.random.fold_in(key_of[7], 71), 0),
        "q_gain": draw_q_gain(jax.random.fold_in(key_of[7], 71), 0),
        "w_out": bell_draw(key_of[6], (HEADS * HD, D), (HEADS * HD) ** -0.5, 0.1875, ((0, 64),)),
    }


def embed(levels):
    half = FREQ // 2
    freqs = jnp.exp(-math.log(10000.0) * jnp.arange(half, dtype=jnp.float32) / half)
    angles = levels.astype(jnp.float32)[:, None] * freqs[None, :]
    return jnp.concatenate([jnp.cos(angles), jnp.sin(angles)], axis=1).astype(jnp.bfloat16)

def alpha_bar(steps):
    frac = steps.astype(jnp.float32) / LEVELS
    return jnp.cos((frac + 0.008) / 1.008 * (math.pi / 2)) ** 2

def reference(frames_in, levels, fresh, w_mod, w_qkv, q_gain, w_out):
    mod = jnp.dot(embed(levels), w_mod, preferred_element_type=jnp.float32)
    shift = mod[:, :D]
    scale = mod[:, D:]
    x32 = frames_in.astype(jnp.float32)
    mean = lax.optimization_barrier(jnp.mean(x32, axis=-1, keepdims=True))
    var = lax.optimization_barrier(jnp.mean((x32 - mean) ** 2, axis=-1, keepdims=True))
    normed = (x32 - mean) * lax.rsqrt(var + 1e-06)
    xm = (normed * (1.0 + scale[:, None, :]) + shift[:, None, :]).astype(jnp.bfloat16)

    def project(rows):
        qkv = jnp.dot(rows, w_qkv, preferred_element_type=jnp.float32).reshape(TOKENS, 3, HEADS, HD)
        query = qkv[:, 0]
        key = qkv[:, 1]
        query = query * lax.rsqrt(lax.optimization_barrier(jnp.mean(query * query, axis=-1, keepdims=True)) + 1e-06) * q_gain[None, :, None]
        key = key * lax.rsqrt(lax.optimization_barrier(jnp.mean(key * key, axis=-1, keepdims=True)) + 1e-06)
        return (query.astype(jnp.bfloat16), key.astype(jnp.bfloat16), qkv[:, 2].astype(jnp.bfloat16))
    queries, keys, values = lax.map(project, xm)
    blocks = TOKENS // HALF
    inv = 1.0 / math.sqrt(HD)
    kk = jnp.arange(3 * HALF)[None, :]
    rr = jnp.arange(HALF)[:, None]
    band = jnp.abs(kk - rr - HALF) <= HALF
    order = jnp.arange(FRAMES)
    v_all = values.astype(jnp.float32).reshape(FRAMES, blocks, HALF, HEADS, HD)
    k_all = keys.astype(jnp.float32)
    results = []
    for frame in range(FRAMES):
        qb = queries[frame].astype(jnp.float32).reshape(blocks, HALF, HEADS, HD)
        kb = keys[frame].astype(jnp.float32).reshape(blocks, HALF, HEADS, HD)
        vb = values[frame].astype(jnp.float32).reshape(blocks, HALF, HEADS, HD)
        kwin = jnp.concatenate([jnp.roll(kb, 1, axis=0), kb, jnp.roll(kb, -1, axis=0)], axis=1)
        vwin = jnp.concatenate([jnp.roll(vb, 1, axis=0), vb, jnp.roll(vb, -1, axis=0)], axis=1)
        spatial = jnp.einsum('brhd,bkhd->bhrk', qb, kwin) * inv
        spatial = jnp.where(band[None, None], spatial, -1e+30)
        temporal = jnp.einsum('thd,gthd->thg', queries[frame].astype(jnp.float32), k_all) * inv
        causal = order < frame
        temporal = jnp.where(causal[None, None, :], temporal, -1e+30)
        temporal = temporal.reshape(blocks, HALF, HEADS, FRAMES).transpose(0, 2, 1, 3)
        top = jnp.maximum(lax.optimization_barrier(jnp.max(spatial, axis=-1)), lax.optimization_barrier(jnp.max(temporal, axis=-1)))
        p_space = jnp.where(band[None, None], jnp.exp(spatial - top[..., None]), 0.0)
        p_time = jnp.where(causal[None, None, None, :], jnp.exp(temporal - top[..., None]), 0.0)
        total = lax.optimization_barrier(jnp.sum(p_space, axis=-1)) + lax.optimization_barrier(jnp.sum(p_time, axis=-1))
        acc = jnp.einsum('bhrk,bkhd->brhd', p_space.astype(jnp.bfloat16).astype(jnp.float32), vwin)
        acc = acc + jnp.einsum('bhrg,gbrhd->brhd', p_time.astype(jnp.bfloat16).astype(jnp.float32), v_all)
        attended = (acc / total.transpose(0, 2, 1)[..., None]).astype(jnp.bfloat16).reshape(TOKENS, HEADS * HD)
        eps = x32[frame] + jnp.dot(attended, w_out, preferred_element_type=jnp.float32)
        now = levels[frame]
        later = jnp.maximum(now - LEVELS // FRAMES, 0)
        a_now = alpha_bar(now)
        a_later = alpha_bar(later)
        clean = (x32[frame] - jnp.sqrt(1.0 - a_now) * eps) / jnp.sqrt(a_now)
        results.append((jnp.sqrt(a_later) * clean + jnp.sqrt(1.0 - a_later) * eps).astype(jnp.bfloat16))
    return jnp.stack(results[1:] + [fresh], axis=0)
```

```python
import functools
import math

import jax
import jax.numpy as jnp
from jax import lax
from jax.experimental import pallas as pl
from jax.experimental.pallas import tpu as pltpu
from jax.sharding import Mesh, PartitionSpec as P

LEVELS = 1000
FRAMES = 8
F32 = jnp.float32
BF16 = jnp.bfloat16
AXES = ("yl", "core", "x", "yh", "z")
SIZES = (2, 2, 4, 2, 8)
SIZE = dict(zip(AXES, SIZES))
VMEM_LIMIT = 48 * 1024 * 1024


def embed(levels, freq_count):
    half = freq_count // 2
    freqs = jnp.exp(-math.log(10000.0) * jnp.arange(half, dtype=F32) / half)
    angles = levels.astype(F32)[:, None] * freqs[None, :]
    return jnp.concatenate([jnp.cos(angles), jnp.sin(angles)], axis=1).astype(BF16)


def alpha_bar(steps):
    frac = steps.astype(F32) / LEVELS
    return jnp.cos((frac + 0.008) / 1.008 * (math.pi / 2)) ** 2


def swap(array, axis):
    return lax.ppermute(array, axis, [(0, 1), (1, 0)])


def both_ways(array, axis, by):
    n = SIZE[axis]
    pairs = [(i, (i + by) % n) for i in range(n)]
    pairs += [(n + i, n + (i - by) % n) for i in range(n)]
    return lax.ppermute(array, ("core", axis), pairs)


def pick(array, index, axis=0):
    return lax.dynamic_index_in_dim(array, index, axis, keepdims=False)


def call(body, out_shape, scalars, arrays, scratch=(), flops=0):
    specs = [pl.BlockSpec(memory_space=pltpu.SMEM)] * len(scalars)
    specs += [pl.BlockSpec(memory_space=pltpu.VMEM)] * len(arrays)
    moved = sum(a.size * a.dtype.itemsize for a in arrays)
    moved += sum(math.prod(s.shape) * s.dtype.itemsize for s in jax.tree.leaves(out_shape))
    return pl.pallas_call(
        body,
        out_shape=out_shape,
        in_specs=specs,
        out_specs=jax.tree.map(lambda _: pl.BlockSpec(memory_space=pltpu.VMEM), out_shape),
        scratch_shapes=list(scratch),
        compiler_params=pltpu.CompilerParams(vmem_limit_bytes=VMEM_LIMIT),
        cost_estimate=pl.CostEstimate(flops=flops, bytes_accessed=moved, transcendentals=0),
    )(*scalars, *arrays)


def norm_kernel(x_ref, shift_ref, scale_ref, out_ref):
    frames, rows, width = x_ref.shape
    chunk = 32
    for f in range(frames):
        shift = shift_ref[f][None]
        scale = 1.0 + scale_ref[f][None]

        @pl.loop(0, rows // chunk)
        def _(step):
            at = pl.ds(pl.multiple_of(step * chunk, chunk), chunk)
            x = x_ref[f, at, :].astype(F32)
            mean = jnp.mean(x, axis=-1, keepdims=True)
            x = x - mean
            var = jnp.mean(x * x, axis=-1, keepdims=True)
            out_ref[f, at, :] = (x * lax.rsqrt(var + 1e-06) * scale + shift).astype(BF16)


def norm_rows(x, shift, scale):
    return call(norm_kernel, jax.ShapeDtypeStruct(x.shape, BF16), (), (x, shift, scale), flops=20 * x.size)


def place_z_kernel(ids, own_ref, r1, r2, r3, r4, s1, s2, s3, s4, k_ref, q_ref):
    c, sign, zi = ids[0], ids[1], ids[2]
    outs = (k_ref, q_ref)

    def put(ref, z):
        for part in range(2):
            outs[part][:, :, pl.ds(z, 1)] = ref[:, part][:, :, None]

    put(own_ref, zi)
    for by, (mine, other) in enumerate(((r1, s1), (r2, s2), (r3, s3)), 1):
        put(mine, lax.rem(zi - sign * by + 8, 8))
        put(other, lax.rem(zi + sign * by + 8, 8))
    far = lax.rem(zi + 4, 8)
    for part in range(2):
        outs[part][pl.ds(c, 1), :, pl.ds(far, 1)] = r4[part][None, :, None]
        outs[part][pl.ds(1 - c, 1), :, pl.ds(far, 1)] = s4[part][None, :, None]


def place_x_kernel(ids, own_ref, r1, r2, s1, s2, v_ref):
    c, sign, xi = ids[0], ids[1], ids[3]
    v_ref[pl.ds(xi, 1)] = own_ref[...][None]
    v_ref[pl.ds(lax.rem(xi - sign + 4, 4), 1)] = r1[...][None]
    v_ref[pl.ds(lax.rem(xi + sign + 4, 4), 1)] = s1[...][None]
    far = lax.rem(xi + 2, 4)
    v_ref[pl.ds(far, 1), pl.ds(c, 1)] = r2[...][None, None]
    v_ref[pl.ds(far, 1), pl.ds(1 - c, 1)] = s2[...][None, None]


def weight_from_x(ids, refs, w_ref):
    own_ref, r1, r2, s1, s2 = refs
    c, sign, xi = ids[0], ids[1], ids[3]
    w_ref[pl.ds(xi, 1)] = own_ref[:, pl.ds(c, 1)].reshape(1, 2, 8, 32, 256)
    w_ref[pl.ds(lax.rem(xi - sign + 4, 4), 1)] = r1[:, pl.ds(c, 1)].reshape(1, 2, 8, 32, 256)
    w_ref[pl.ds(lax.rem(xi + sign + 4, 4), 1)] = s1[...][None]
    far = lax.rem(xi + 2, 4)
    w_ref[pl.ds(far, 1), pl.ds(c, 1)] = r2[pl.ds(c, 1)][None]
    w_ref[pl.ds(far, 1), pl.ds(1 - c, 1)] = s2[...][None, None]


def weight_from_z(ids, refs, w_ref):
    own_ref, r1, r2, r3, r4, s1, s2, s3, s4 = refs
    c, sign, zi = ids[0], ids[1], ids[2]
    w_ref[:, :, pl.ds(zi, 1)] = own_ref[:, :, pl.ds(c, 1)]
    for by, (mine, other) in enumerate(((r1, s1), (r2, s2), (r3, s3)), 1):
        w_ref[:, :, pl.ds(lax.rem(zi - sign * by + 8, 8), 1)] = mine[:, :, pl.ds(c, 1)]
        w_ref[:, :, pl.ds(lax.rem(zi + sign * by + 8, 8), 1)] = other[...][:, :, None]
    far = lax.rem(zi + 4, 8)
    w_ref[pl.ds(2 * c, 2), :, pl.ds(far, 1)] = r4[:, :, pl.ds(c, 1)]
    w_ref[pl.ds(2 - 2 * c, 2), :, pl.ds(far, 1)] = s4[...][:, :, None]


def project_kernel(gather, normed, ids, gains, *refs):
    *pieces, x0, x1, x2, x3, out_ref, w_ref = refs
    gather(ids, pieces, w_ref)
    weight = w_ref[...].reshape(2048, 256)
    for group, x_ref in enumerate((x0, x1, x2, x3)):
        first = ids[4 + group]
        got = jnp.dot(x_ref[...].reshape(256, 2048), weight, preferred_element_type=F32)
        if normed:
            heads = []
            for h in range(2):
                part = got[:, h * 128 : (h + 1) * 128]
                part = part * lax.rsqrt(jnp.mean(part * part, axis=-1, keepdims=True) + 1e-06)
                heads.append(part * gains[h])
            got = jnp.concatenate(heads, axis=1)
        out_ref[pl.ds(first, 2)] = got.astype(BF16).reshape(2, 128, 256)


def project(ids, gains, pieces, xs, gather, normed):
    return call(
        functools.partial(project_kernel, gather, normed),
        jax.ShapeDtypeStruct((FRAMES, 128, 256), BF16),
        (ids, gains),
        (*pieces, *xs),
        scratch=[pltpu.VMEM((4, 2, 8, 32, 256), BF16)],
        flops=2 * 1024 * 2048 * 256,
    )


def attend_kernel(q_ref, k_ref, v_ref, kl_ref, kr_ref, vl_ref, vr_ref, out_ref):
    inv = 1.0 / math.sqrt(128)
    rr = lax.broadcasted_iota(jnp.int32, (128, 128), 0)
    kk = lax.broadcasted_iota(jnp.int32, (128, 128), 1)
    in_left = kk >= rr
    in_right = kk <= rr
    nt = (((1,), (1,)), ((), ()))
    for f in range(1, FRAMES):
        for h in range(2):
            lanes = slice(h * 128, (h + 1) * 128)
            q = q_ref[f, :, lanes]
            left = lax.dot_general(q, kl_ref[f - 1, :, lanes], nt, preferred_element_type=F32) * inv
            mid = lax.dot_general(q, k_ref[f, :, lanes], nt, preferred_element_type=F32) * inv
            right = lax.dot_general(q, kr_ref[f - 1, :, lanes], nt, preferred_element_type=F32) * inv
            left = jnp.where(in_left, left, -1e30)
            right = jnp.where(in_right, right, -1e30)
            q32 = q.astype(F32)
            earlier = [
                jnp.sum(q32 * k_ref[g, :, lanes].astype(F32), axis=-1, keepdims=True) * inv
                for g in range(f)
            ]
            top = jnp.max(jnp.maximum(jnp.maximum(left, mid), right), axis=-1, keepdims=True)
            for score in earlier:
                top = jnp.maximum(top, score)
            left = jnp.where(in_left, jnp.exp(left - top), 0.0)
            mid = jnp.exp(mid - top)
            right = jnp.where(in_right, jnp.exp(right - top), 0.0)
            total = jnp.sum(left + mid + right, axis=-1, keepdims=True)
            acc = jnp.dot(left.astype(BF16), vl_ref[f - 1, :, lanes], preferred_element_type=F32)
            acc += jnp.dot(mid.astype(BF16), v_ref[f, :, lanes], preferred_element_type=F32)
            acc += jnp.dot(right.astype(BF16), vr_ref[f - 1, :, lanes], preferred_element_type=F32)
            for g, score in enumerate(earlier):
                p = jnp.exp(score - top)
                total += p
                acc += p.astype(BF16).astype(F32) * v_ref[g, :, lanes].astype(F32)
            out_ref[f - 1, :, lanes] = (acc / total).astype(BF16)
    out_ref[FRAMES - 1] = jnp.zeros_like(out_ref[FRAMES - 1])


def finish_kernel(ids, coefs, o_ref, wa_ref, wb_ref, x0_ref, x1_ref, fresh_ref, out_ref):
    c, last = ids[0], ids[8]
    for which, w_ref in enumerate((wa_ref, wb_ref)):
        side = c if which == 0 else 1 - c
        columns = pl.ds(pl.multiple_of(side * 1024, 1024), 1024)
        eps = None
        for s in range(4):
            weight = jnp.concatenate(
                [w_ref[s, :, yh].reshape(128, 1024) for yh in range(2)], axis=0
            )
            term = jnp.dot(o_ref[s].reshape(256, 256), weight, preferred_element_type=F32)
            eps = term if eps is None else eps + term
        for slot, x_ref in enumerate((x0_ref, x1_ref)):
            x = x_ref[:, columns].astype(F32)
            e = x + eps[slot * 128 : (slot + 1) * 128]
            done = coefs[4 * slot] * ((x - coefs[4 * slot + 1] * e) * coefs[4 * slot + 2])
            done = (done + coefs[4 * slot + 3] * e).astype(BF16)
            if slot == 1:
                done = jnp.where(last == 1, fresh_ref[:, columns], done)
            out_ref[slot, :, columns] = done


def body(frames_in, levels, fresh, w_mod, w_qkv, q_gain, w_out):
    width = frames_in.shape[2]
    yl, c = lax.axis_index("yl"), lax.axis_index("core")
    xi, yhi, zi = lax.axis_index("x"), lax.axis_index("yh"), lax.axis_index("z")
    me = 2 * yl + c
    groups = (me, 2 * yl + 1 - c, 2 * (1 - yl) + c, 2 * (1 - yl) + 1 - c)
    ids = jnp.stack(
        [c, 1 - 2 * c, zi, xi, *(2 * g for g in groups), (me == 3).astype(jnp.int32)]
    ).astype(jnp.int32)
    gains = lax.dynamic_slice(q_gain, (2 * me,), (2,))
    ones = jnp.ones((2,), F32)

    mine = pick(w_qkv.reshape(32, 3, 2, 2, 256), yl, 2).transpose(1, 2, 0, 3)
    mine = jnp.stack([mine[2], mine[1], mine[0]]).reshape(192, 256)
    half = lax.dynamic_slice(w_out, (0, 1024 * c), (16, 1024)).reshape(64, 256)
    pack = jnp.concatenate([mine, half], axis=0)
    got = swap(pack, "yh")
    pair = jnp.stack([jnp.where(yhi == 0, pack, got), jnp.where(yhi == 0, got, pack)])
    out_half = lax.all_gather(pair[:, 192:].reshape(32, 1024), ("x", "z"), axis=0, tiled=True)
    pair = pair[:, :192].reshape(2, 3, 2, 32, 256)
    value, rest = pair[:, 0], pair[:, 1:]

    mod = jnp.dot(embed(levels, w_mod.shape[0]), w_mod, preferred_element_type=F32)
    own = norm_rows(frames_in, mod[:, :width], mod[:, width:])
    across = swap(own, "yl")
    beside = swap(own, "core")
    diagonal = swap(across, "core")
    xs = (own, beside, across, diagonal)

    a1 = both_ways(value, "x", 1)
    a2 = both_ways(pick(value, c), "x", 2)
    block = call(
        place_x_kernel,
        jax.ShapeDtypeStruct((4, 2, 2, 32, 256), BF16),
        (ids,),
        (value, a1, a2, swap(a1, "core"), swap(a2, "core")),
    )
    r1 = both_ways(block, "z", 1)
    r2 = both_ways(r1, "z", 1)
    r3 = both_ways(r2, "z", 1)
    r4 = both_ways(lax.dynamic_slice_in_dim(r3, 2 * c, 2, 0), "z", 1)
    sent = [swap(pick(r, 1 - c, 2), "core") for r in (r1, r2, r3, r4)]
    values = project(ids, ones, (block, r1, r2, r3, r4, *sent), xs, weight_from_z, False)

    b = [both_ways(rest, "z", by) for by in (1, 2, 3)]
    b.append(both_ways(pick(rest, c), "z", 4))
    k_block, q_block = call(
        place_z_kernel,
        [jax.ShapeDtypeStruct((2, 2, 8, 32, 256), BF16)] * 2,
        (ids,),
        (rest, *b, *(swap(t, "core") for t in b)),
    )

    def round_x(block):
        r1 = both_ways(block, "x", 1)
        r2 = both_ways(pick(r1, c), "x", 1)
        return block, r1, r2, swap(pick(r1, 1 - c, 1), "core"), swap(pick(r2, 1 - c), "core")

    keys = project(ids, ones, round_x(k_block), xs, weight_from_x, True)
    queries = project(ids, gains, round_x(q_block), xs, weight_from_x, True)

    ring = ("x", "yh", "z")
    up = [(i, (i + 1) % 64) for i in range(64)]
    down = [((i + 1) % 64, i) for i in range(64)]
    vl, vr = lax.ppermute(values[1:], ring, up), lax.ppermute(values[1:], ring, down)
    kl, kr = lax.ppermute(keys[1:], ring, up), lax.ppermute(keys[1:], ring, down)
    o = call(
        attend_kernel,
        jax.ShapeDtypeStruct((FRAMES, 128, 256), BF16),
        (),
        (queries, keys, values, kl, kr, vl, vr),
        flops=14 * 6 * 2 * 128 * 128 * 128,
    )
    o = lax.all_to_all(o.reshape(4, 2, 128, 256), ("yl", "core"), 0, 0)

    back = [(i + 1, i) for i in range(3)]
    next_x = lax.ppermute(frames_in[0], ("yl", "core"), back)
    next_level = lax.ppermute(levels[:1], ("yl", "core"), back)
    now = jnp.concatenate([levels[1:], next_level])
    a_now = alpha_bar(now)
    a_later = alpha_bar(jnp.maximum(now - LEVELS // FRAMES, 0))
    coefs = jnp.stack(
        [jnp.sqrt(a_later), jnp.sqrt(1.0 - a_now), 1.0 / jnp.sqrt(a_now), jnp.sqrt(1.0 - a_later)],
        axis=1,
    ).reshape(8)
    out_half = out_half.reshape(4, 8, 2, 16, 1024)
    return call(
        finish_kernel,
        jax.ShapeDtypeStruct(frames_in.shape, BF16),
        (ids, coefs),
        (o, out_half, swap(out_half, "core"), frames_in[1], next_x, fresh),
        flops=2 * 256 * 1024 * 2048,
    )


def solution(mesh):
    cut = Mesh(mesh.devices.reshape(SIZES), AXES)
    frame, space = ("yl", "core"), ("x", "yh", "z")
    return jax.shard_map(
        body,
        mesh=cut,
        in_specs=(
            P(frame, space, None),
            P(frame),
            P(space, None),
            P(),
            P(space, None),
            P(),
            P(space, None),
        ),
        out_specs=P(frame, space, None),
        check_vma=False,
    )
```

```python
import functools
import math

import jax
import jax.numpy as jnp
from jax import lax
from jax.experimental import pallas as pl
from jax.experimental.pallas import tpu as pltpu
from jax.sharding import Mesh, PartitionSpec as P

LEVELS = 1000
FRAMES = 8
F32 = jnp.float32
BF16 = jnp.bfloat16
AXES = ("yl", "core", "x", "yh", "z")
SIZES = (2, 2, 4, 2, 8)
SIZE = dict(zip(AXES, SIZES))
PLACES = (0, 3, 1, 2)
VMEM_LIMIT = 20 * 1024 * 1024


def embed(levels, freq_count):
    half = freq_count // 2
    freqs = jnp.exp(-math.log(10000.0) * jnp.arange(half, dtype=F32) / half)
    angles = levels.astype(F32)[:, None] * freqs[None, :]
    return jnp.concatenate([jnp.cos(angles), jnp.sin(angles)], axis=1).astype(BF16)


def alpha_bar(steps):
    frac = steps.astype(F32) / LEVELS
    return jnp.cos((frac + 0.008) / 1.008 * (math.pi / 2)) ** 2


def swap(array, axis):
    return lax.ppermute(array, axis, [(0, 1), (1, 0)])


def shift(array, axis, by):
    n = SIZE[axis]
    return lax.ppermute(array, axis, [(i, (i + by) % n) for i in range(n)])


def after(array, *others):
    return lax.optimization_barrier((array, *others))[0]


def gather(array, axis):
    copies = lax.optimization_barrier(jnp.broadcast_to(array[None], (SIZE[axis], *array.shape)))
    return lax.all_to_all(copies, axis, 0, 0)


def call(body, out_shape, scalars, far, near=(), scratch=()):
    specs = [pl.BlockSpec(memory_space=pltpu.SMEM)] * len(scalars)
    specs += [pl.BlockSpec(memory_space=pltpu.HBM)] * len(far)
    specs += [pl.BlockSpec(memory_space=pltpu.VMEM)] * len(near)
    return pl.pallas_call(
        body,
        out_shape=out_shape,
        in_specs=specs,
        out_specs=jax.tree.map(lambda _: pl.BlockSpec(memory_space=pltpu.VMEM), out_shape),
        scratch_shapes=list(scratch),
        compiler_params=pltpu.CompilerParams(vmem_limit_bytes=VMEM_LIMIT),
        cost_estimate=pl.CostEstimate(flops=0, bytes_accessed=0, transcendentals=0),
    )(*scalars, *far, *near)


def norm_kernel(x_ref, shift_ref, scale_ref, out_ref, copy_ref):
    copy_ref[...] = x_ref[0]
    frames, rows, width = x_ref.shape
    chunk = 32
    for f in range(frames):
        shift = shift_ref[f][None]
        scale = 1.0 + scale_ref[f][None]

        @pl.loop(0, rows // chunk)
        def _(step):
            at = pl.ds(pl.multiple_of(step * chunk, chunk), chunk)
            x = x_ref[f, at, :].astype(F32)
            mean = jnp.mean(x, axis=-1, keepdims=True)
            x = x - mean
            var = jnp.mean(x * x, axis=-1, keepdims=True)
            out_ref[f, at, :] = (x * lax.rsqrt(var + 1e-06) * scale + shift).astype(BF16)


def norm_rows(x, shift, scale):
    shapes = [jax.ShapeDtypeStruct(x.shape, BF16), jax.ShapeDtypeStruct(x.shape[1:], BF16)]
    return call(norm_kernel, shapes, (), (), (x, shift, scale))


def project_kernel(ids, gains, *refs):
    *pieces, late, x0, x1, x2, x3, first_ref, out_ref, q_ref, w_ref, x_ref, sems = refs
    copies = [(ref, x_ref.at[pl.ds(ids[4 + group], 2)]) for group, ref in enumerate((x0, x1, x2, x3))]
    for place, by in enumerate(PLACES):
        x = lax.rem(ids[3] + by, 4)
        for yh in range(2):
            copies.append((pieces[place].at[:, yh, :32], w_ref.at[0, x, yh]))
            copies.append((pieces[place].at[:, yh, 32:], w_ref.at[1, x, yh]))
            copies.append((late.at[:, place, yh, :32], w_ref.at[2, x, yh]))
    copies = [pltpu.make_async_copy(a, b, sems.at[i]) for i, (a, b) in enumerate(copies)]
    for copy in copies:
        copy.start()
    for copy in copies:
        copy.wait()
    for part in range(3):
        weight = w_ref[part].reshape(2048, 256)
        for f in range(0, FRAMES, 4):
            rows = x_ref[f : f + 4].reshape(512, 2048)
            got = jnp.dot(rows, weight, preferred_element_type=F32)
            if part != 1:
                heads = []
                for h in range(2):
                    one = got[:, h * 128 : (h + 1) * 128]
                    one = one * lax.rsqrt(jnp.mean(one * one, axis=-1, keepdims=True) + 1e-06)
                    heads.append(one * gains[h] if part == 2 else one)
                got = jnp.concatenate(heads, axis=1)
            got = got.astype(BF16)
            if part < 2 and f == 0:
                first_ref[part] = got[:128]
                out_ref[:3, part] = got[128:].reshape(3, 128, 256)
            elif part < 2:
                out_ref[3:, part] = got.reshape(4, 128, 256)
            else:
                q_ref[f : f + 4] = got.reshape(4, 128, 256)


def project(ids, gains, pieces, late, xs):
    return call(
        project_kernel,
        [
            jax.ShapeDtypeStruct((2, 128, 256), BF16),
            jax.ShapeDtypeStruct((FRAMES - 1, 2, 128, 256), BF16),
            jax.ShapeDtypeStruct((FRAMES, 128, 256), BF16),
        ],
        (ids, gains),
        (*pieces, late, *xs),
        scratch=[
            pltpu.VMEM((3, 4, 2, 8, 32, 256), BF16),
            pltpu.VMEM((FRAMES, 128, 2048), BF16),
            pltpu.SemaphoreType.DMA((28,)),
        ],
    )


def attend_kernel(q_ref, first_ref, kv_ref, left_ref, right_ref, out_ref):
    inv = 1.0 / math.sqrt(128)
    rr = lax.broadcasted_iota(jnp.int32, (128, 128), 0)
    kk = lax.broadcasted_iota(jnp.int32, (128, 128), 1)
    in_left = kk >= rr
    in_right = kk <= rr
    nt = (((1,), (1,)), ((), ()))

    def frame(g, part, lanes):
        return (first_ref[part, :, lanes] if g == 0 else kv_ref[g - 1, part, :, lanes]).astype(F32)

    for f in range(1, FRAMES):
        for h in range(2):
            lanes = slice(h * 128, (h + 1) * 128)
            q = q_ref[f, :, lanes]
            left, mid, right = (
                lax.dot_general(q, ref[f - 1, 0, :, lanes], nt, preferred_element_type=F32) * inv
                for ref in (left_ref, kv_ref, right_ref)
            )
            left = jnp.where(in_left, left, -1e30)
            right = jnp.where(in_right, right, -1e30)
            q32 = q.astype(F32)
            earlier = [
                jnp.sum(q32 * frame(g, 0, lanes), axis=-1, keepdims=True) * inv for g in range(f)
            ]
            top = jnp.max(jnp.maximum(jnp.maximum(left, mid), right), axis=-1, keepdims=True)
            for score in earlier:
                top = jnp.maximum(top, score)
            left = jnp.where(in_left, jnp.exp(left - top), 0.0)
            mid = jnp.exp(mid - top)
            right = jnp.where(in_right, jnp.exp(right - top), 0.0)
            total = jnp.sum(left + mid + right, axis=-1, keepdims=True)
            acc = None
            for p, ref in ((left, left_ref), (mid, kv_ref), (right, right_ref)):
                term = jnp.dot(p.astype(BF16), ref[f - 1, 1, :, lanes], preferred_element_type=F32)
                acc = term if acc is None else acc + term
            for g, score in enumerate(earlier):
                p = jnp.exp(score - top)
                total += p
                acc += p.astype(BF16).astype(F32) * frame(g, 1, lanes)
            out_ref[f - 1, :, lanes] = (acc / total).astype(BF16)
    out_ref[FRAMES - 1] = jnp.zeros_like(out_ref[FRAMES - 1])


def finish_kernel(ids, coefs, wa_hbm, wb_hbm, x0_hbm, x1_hbm, fresh_hbm, o_ref, out_ref, w_ref, x_ref, sems, x_sems):
    c, last = ids[0], ids[8]
    copies = {}
    for which, hbm in enumerate((wa_hbm, wb_hbm)):
        for place in range(4):
            copies[which, place] = pltpu.make_async_copy(
                hbm.at[:, place, :, 32:96], w_ref.at[which, place], sems.at[which, place]
            )
            copies[which, place].start()
        if which == 0:
            rows = [
                pltpu.make_async_copy(hbm, x_ref.at[i], x_sems.at[i])
                for i, hbm in enumerate((x0_hbm.at[1], x1_hbm, fresh_hbm))
            ]
            for copy in rows:
                copy.start()
    for which in range(2):
        side = c if which == 0 else 1 - c
        eps = [None] * 4
        for place, by in enumerate(PLACES):
            copies[which, place].wait()
            o = o_ref[pl.ds(lax.rem(ids[3] + by, 4), 1)].reshape(256, 256)
            for part in range(4):
                weight = jnp.concatenate(
                    [
                        w_ref[which, place, :, yh, 16 * part : 16 * part + 16].reshape(128, 256)
                        for yh in range(2)
                    ],
                    axis=0,
                )
                term = jnp.dot(o, weight, preferred_element_type=F32)
                eps[part] = term if place == 0 else eps[part] + term
        if which == 0:
            for copy in rows:
                copy.wait()
        for part in range(4):
            columns = pl.ds(pl.multiple_of(side * 1024 + part * 256, 256), 256)
            for slot in range(2):
                x = x_ref[slot, :, columns].astype(F32)
                e = x + eps[part][slot * 128 : (slot + 1) * 128]
                done = coefs[4 * slot] * ((x - coefs[4 * slot + 1] * e) * coefs[4 * slot + 2])
                done = (done + coefs[4 * slot + 3] * e).astype(BF16)
                if slot == 1:
                    done = jnp.where(last == 1, x_ref[2, :, columns], done)
                out_ref[slot, :, columns] = done


def body(frames_in, levels, fresh, w_mod, w_qkv, q_gain, w_out):
    width = frames_in.shape[2]
    yl, c = lax.axis_index("yl"), lax.axis_index("core")
    xi, yhi, zi = lax.axis_index("x"), lax.axis_index("yh"), lax.axis_index("z")
    me = 2 * yl + c
    groups = (me, 2 * yl + 1 - c, 2 * (1 - yl) + c, 2 * (1 - yl) + 1 - c)
    ids = jnp.stack(
        [c, 1 - 2 * c, zi, xi, *(2 * g for g in groups), (me == 3).astype(jnp.int32)]
    ).astype(jnp.int32)
    gains = lax.dynamic_slice(q_gain, (2 * me,), (2,))

    columns = [lax.dynamic_slice(w_qkv, (0, 1024 * part + 256 * me), (32, 256)) for part in (1, 2, 0)]
    half = lax.dynamic_slice(w_out, (0, 1024 * c), (16, 1024))
    half = half.reshape(16, 4, 256).transpose(1, 0, 2).reshape(64, 256)
    pack = jnp.concatenate([*columns, half], axis=0)
    back = [(i + 1, i) for i in range(3)]
    next_level = lax.ppermute(levels[:1], ("yl", "core"), back)
    other = swap(pack, "yh")
    pair = jnp.stack([jnp.where(yhi == 0, pack, other), jnp.where(yhi == 0, other, pack)])

    mod = jnp.dot(embed(levels, w_mod.shape[0]), w_mod, preferred_element_type=F32)
    own, first_x = norm_rows(frames_in, mod[:, :width], mod[:, width:])
    pair, own, next_level = lax.optimization_barrier((pair, own, next_level))
    across = swap(own, "yl")
    beside = swap(own, "core")

    def along_x(block):
        return block, shift(block, "x", 1), shift(block, "x", -1), shift(block, "x", 2)

    late = along_x(pair[:, 64:])
    block = gather(pair[:, :64], "z")
    late = lax.all_gather(jnp.stack(late), "z", axis=0)
    block, across, beside = lax.optimization_barrier((block, across, beside))
    pieces = along_x(block)
    diagonal = swap(across, "core")
    next_x = lax.ppermute(after(first_x, block), ("yl", "core"), back)
    diagonal, next_x, *pieces = lax.optimization_barrier((diagonal, next_x, *pieces))
    xs = (own, beside, across, diagonal)

    line = ("x", "yh", "z")
    right = [(i, (i + 1) % 64) for i in range(64)]
    left = [((i + 1) % 64, i) for i in range(64)]
    first, here, queries = project(ids, gains, pieces, late, xs)
    from_left, from_right = lax.ppermute(here, line, right), lax.ppermute(here, line, left)

    mine = call(
        attend_kernel,
        jax.ShapeDtypeStruct((FRAMES, 128, 256), BF16),
        (),
        (),
        (queries, first, here, from_left, from_right),
    )
    o = lax.all_to_all(mine.reshape(4, 2, 128, 256), ("yl", "core"), 0, 0)

    now = jnp.concatenate([levels[1:], next_level])
    a_now = alpha_bar(now)
    a_later = alpha_bar(jnp.maximum(now - LEVELS // FRAMES, 0))
    coefs = jnp.stack(
        [jnp.sqrt(a_later), jnp.sqrt(1.0 - a_now), 1.0 / jnp.sqrt(a_now), jnp.sqrt(1.0 - a_later)],
        axis=1,
    ).reshape(8)
    return call(
        finish_kernel,
        jax.ShapeDtypeStruct(frames_in.shape, BF16),
        (ids, coefs),
        (late, swap(after(late, mine), "core"), frames_in, next_x, fresh),
        (o,),
        scratch=[
            pltpu.VMEM((2, 4, 8, 2, 64, 256), BF16),
            pltpu.VMEM((3, 128, 2048), BF16),
            pltpu.SemaphoreType.DMA((2, 4)),
            pltpu.SemaphoreType.DMA((3,)),
        ],
    )


def solution(mesh):
    cut = Mesh(mesh.devices.reshape(SIZES), AXES)
    frame, space = ("yl", "core"), ("x", "yh", "z")
    return jax.shard_map(
        body,
        mesh=cut,
        in_specs=(
            P(frame, space, None),
            P(frame),
            P(space, None),
            P(),
            P(space, None),
            P(),
            P(space, None),
        ),
        out_specs=P(frame, space, None),
        check_vma=False,
    )
```

```python
import functools
import math

import jax
import jax.numpy as jnp
from jax import lax
from jax.experimental import pallas as pl
from jax.experimental.pallas import tpu as pltpu
from jax.sharding import Mesh, PartitionSpec as P

LEVELS = 1000
FRAMES = 8
F32 = jnp.float32
BF16 = jnp.bfloat16
AXES = ("yl", "core", "x", "yh", "z")
SIZES = (2, 2, 4, 2, 8)
SIZE = dict(zip(AXES, SIZES))
NEAR_LIMIT = 20 * 1024 * 1024
FAR_LIMIT = 56 * 1024 * 1024


def embed(levels, freq_count):
    half = freq_count // 2
    freqs = jnp.exp(-math.log(10000.0) * jnp.arange(half, dtype=F32) / half)
    angles = levels.astype(F32)[:, None] * freqs[None, :]
    return jnp.concatenate([jnp.cos(angles), jnp.sin(angles)], axis=1).astype(BF16)


def alpha_bar(steps):
    frac = steps.astype(F32) / LEVELS
    return jnp.cos((frac + 0.008) / 1.008 * (math.pi / 2)) ** 2


def swap(array, axis):
    return lax.ppermute(array, axis, [(0, 1), (1, 0)])


def shift(array, axis, by):
    n = SIZE[axis]
    return lax.ppermute(array, axis, [(i, (i + by) % n) for i in range(n)])


def after(array, *others):
    return lax.optimization_barrier((array, *others))[0]


def gather(array, axis):
    size = math.prod(SIZE[a] for a in ((axis,) if isinstance(axis, str) else axis))
    copies = lax.optimization_barrier(jnp.broadcast_to(array[None], (size, *array.shape)))
    return lax.all_to_all(copies, axis, 0, 0)


def call(body, out_shape, scalars, far, near=(), scratch=()):
    limit = FAR_LIMIT if far else NEAR_LIMIT
    specs = [pl.BlockSpec(memory_space=pltpu.SMEM)] * len(scalars)
    specs += [pl.BlockSpec(memory_space=pl.ANY)] * len(far)
    specs += [pl.BlockSpec(memory_space=pltpu.VMEM)] * len(near)
    return pl.pallas_call(
        body,
        out_shape=out_shape,
        in_specs=specs,
        out_specs=jax.tree.map(lambda _: pl.BlockSpec(memory_space=pltpu.VMEM), out_shape),
        scratch_shapes=list(scratch),
        compiler_params=pltpu.CompilerParams(vmem_limit_bytes=limit),
        cost_estimate=pl.CostEstimate(flops=0, bytes_accessed=0, transcendentals=0),
    )(*scalars, *far, *near)


def norm_kernel(x_ref, shift_ref, scale_ref, out_ref, copy_ref):
    copy_ref[...] = x_ref[0]
    frames, rows, width = x_ref.shape
    chunk = 32
    for f in range(frames):
        shift = shift_ref[f][None]
        scale = 1.0 + scale_ref[f][None]

        @pl.loop(0, rows // chunk)
        def _(step):
            at = pl.ds(pl.multiple_of(step * chunk, chunk), chunk)
            x = x_ref[f, at, :].astype(F32)
            mean = jnp.mean(x, axis=-1, keepdims=True)
            x = x - mean
            var = jnp.mean(x * x, axis=-1, keepdims=True)
            out_ref[f, at, :] = (x * lax.rsqrt(var + 1e-06) * scale + shift).astype(BF16)


def norm_rows(x, shift, scale):
    shapes = [jax.ShapeDtypeStruct(x.shape, BF16), jax.ShapeDtypeStruct(x.shape[1:], BF16)]
    return call(norm_kernel, shapes, (), (), (x, shift, scale))


def project_kernel(ids, gains, rows_hbm, x0, x1, x2, x3, first_ref, out_ref, q_ref, w_ref, x_ref, sems):
    copies = [(ref, x_ref.at[pl.ds(ids[4 + group], 2)]) for group, ref in enumerate((x0, x1, x2, x3))]
    copies += [(rows_hbm.at[z], w_ref.at[:, z]) for z in range(8)]
    copies = [pltpu.make_async_copy(a, b, sems.at[i]) for i, (a, b) in enumerate(copies)]
    for copy in copies:
        copy.start()
    for copy in copies:
        copy.wait()
    for part in range(3):
        weight = w_ref[:, :, 32 * part : 32 * part + 32].reshape(2048, 256)
        rows = x_ref[...].reshape(1024, 2048)
        got = jnp.dot(rows, weight, preferred_element_type=F32)
        if part != 1:
            heads = []
            for h in range(2):
                one = got[:, h * 128 : (h + 1) * 128]
                one = one * lax.rsqrt(jnp.mean(one * one, axis=-1, keepdims=True) + 1e-06)
                heads.append(one * gains[h] if part == 2 else one)
            got = jnp.concatenate(heads, axis=1)
        got = got.astype(BF16).reshape(FRAMES, 128, 256)
        if part < 2:
            first_ref[part] = got[0]
            out_ref[:, part] = got[1:]
        else:
            q_ref[...] = got


def project(ids, gains, rows, xs):
    return call(
        project_kernel,
        [
            jax.ShapeDtypeStruct((2, 128, 256), BF16),
            jax.ShapeDtypeStruct((FRAMES - 1, 2, 128, 256), BF16),
            jax.ShapeDtypeStruct((FRAMES, 128, 256), BF16),
        ],
        (ids, gains),
        (rows, *xs),
        scratch=[
            pltpu.VMEM((8, 8, 96, 256), BF16),
            pltpu.VMEM((FRAMES, 128, 2048), BF16),
            pltpu.SemaphoreType.DMA((12,)),
        ],
    )


def attend_kernel(ids, q_ref, first_ref, kv_ref, left_ref, right_ref, o0, o1, o2, o3, out_ref):
    inv = 1.0 / math.sqrt(128)
    rr = lax.broadcasted_iota(jnp.int32, (128, 128), 0)
    kk = lax.broadcasted_iota(jnp.int32, (128, 128), 1)
    in_left = kk >= rr
    in_right = kk <= rr
    nt = (((1,), (1,)), ((), ()))

    def frame(g, part, lanes):
        return (first_ref[part, :, lanes] if g == 0 else kv_ref[g - 1, part, :, lanes]).astype(F32)

    for f in range(1, FRAMES):
        for h in range(2):
            lanes = slice(h * 128, (h + 1) * 128)
            q = q_ref[f, :, lanes]
            left, mid, right = (
                lax.dot_general(q, ref[f - 1, 0, :, lanes], nt, preferred_element_type=F32) * inv
                for ref in (left_ref, kv_ref, right_ref)
            )
            left = jnp.where(in_left, left, -1e30)
            right = jnp.where(in_right, right, -1e30)
            q32 = q.astype(F32)
            earlier = [
                jnp.sum(q32 * frame(g, 0, lanes), axis=-1, keepdims=True) * inv for g in range(f)
            ]
            top = jnp.max(jnp.maximum(jnp.maximum(left, mid), right), axis=-1, keepdims=True)
            for score in earlier:
                top = jnp.maximum(top, score)
            left = jnp.where(in_left, jnp.exp(left - top), 0.0)
            mid = jnp.exp(mid - top)
            right = jnp.where(in_right, jnp.exp(right - top), 0.0)
            total = jnp.sum(left + mid + right, axis=-1, keepdims=True)
            acc = None
            for p, ref in ((left, left_ref), (mid, kv_ref), (right, right_ref)):
                term = jnp.dot(p.astype(BF16), ref[f - 1, 1, :, lanes], preferred_element_type=F32)
                acc = term if acc is None else acc + term
            for g, score in enumerate(earlier):
                p = jnp.exp(score - top)
                total += p
                acc += p.astype(BF16).astype(F32) * frame(g, 1, lanes)
            out_ref[ids[9 + (f - 1) // 2], (f - 1) % 2, :, lanes] = (acc / total).astype(BF16)
    out_ref[ids[12], 1] = jnp.zeros((128, 256), BF16)
    for which, ref in enumerate((o0, o1, o2, o3)):
        ref[...] = out_ref[which]


def finish_kernel(ids, coefs, wa_hbm, wb_hbm, x0_hbm, x1_hbm, fresh_hbm, o0, o1, o2, o3, out_ref, w_ref, x_ref, o_ref, sems, x_sems):
    c, last, yhi = ids[0], ids[8], ids[1]
    rows = [
        pltpu.make_async_copy(hbm, x_ref.at[i], x_sems.at[i])
        for i, hbm in enumerate((x0_hbm.at[1], x1_hbm, fresh_hbm))
    ]
    weights = [
        [
            pltpu.make_async_copy(hbm.at[:, side], w_ref.at[which, :, :, side], sems.at[which, side])
            for side in range(2)
        ]
        for which, hbm in enumerate((wa_hbm, wb_hbm))
    ]
    for copy in (*weights[0], *rows, *weights[1]):
        copy.start()
    for which, ref in enumerate((o0, o1, o2, o3)):
        for h in range(2):
            lanes = ref[:, :, h * 128 : (h + 1) * 128]
            o_ref[pl.ds(2 * ids[9 + which] + h, 1)] = lanes.reshape(1, 256, 128)
    o = [
        jnp.concatenate([o_ref[2 * x + yhi], o_ref[2 * x + 1 - yhi]], axis=1) for x in range(4)
    ]
    for which, part in ((which, part) for which in range(2) for part in range(4)):
        if part == 0:
            for copy in weights[which]:
                copy.wait()
        if which == 0 and part == 0:
            for copy in rows:
                copy.wait()
        start = (c if which == 0 else 1 - c) * 1024 + part * 256
        columns = pl.ds(pl.multiple_of(start, 256), 256)
        eps = None
        for x in range(4):
            weight = w_ref[which, x, part].reshape(256, 256)
            term = jnp.dot(o[x], weight, preferred_element_type=F32)
            eps = term if eps is None else eps + term
        for slot in range(2):
            x = x_ref[slot, :, columns].astype(F32)
            e = x + eps[slot * 128 : (slot + 1) * 128]
            done = coefs[4 * slot] * ((x - coefs[4 * slot + 1] * e) * coefs[4 * slot + 2])
            done = (done + coefs[4 * slot + 3] * e).astype(BF16)
            if slot == 1:
                done = jnp.where(last == 1, x_ref[2, :, columns], done)
            out_ref[slot, :, columns] = done


def body(frames_in, levels, fresh, w_mod, w_qkv, q_gain, w_out):
    width = frames_in.shape[2]
    yl, c = lax.axis_index("yl"), lax.axis_index("core")
    xi, yhi, zi = lax.axis_index("x"), lax.axis_index("yh"), lax.axis_index("z")
    me = 2 * yl + c
    near = [(me ^ k) for k in range(4)]
    ids = jnp.stack([c, yhi, zi, xi, *(2 * g for g in near), me // 3, *near]).astype(jnp.int32)
    gains = lax.dynamic_slice(q_gain, (2 * me,), (2,))

    columns = [lax.dynamic_slice(w_qkv, (0, 1024 * part + 256 * me), (32, 256)) for part in (1, 2, 0)]
    block = gather(jnp.concatenate(columns, axis=0), ("x", "yh"))
    rows = lax.all_gather(block, "z", axis=0)

    mod = jnp.dot(embed(levels, w_mod.shape[0]), w_mod, preferred_element_type=F32)
    own, first_x = norm_rows(frames_in, mod[:, :width], mod[:, width:])
    across = swap(after(own, block), "yl")
    beside = swap(own, "core")

    half = lax.dynamic_slice(w_out, (0, 1024 * c), (16, 1024))
    half = half.reshape(16, 4, 256).transpose(1, 0, 2).reshape(64, 256)
    half = gather(after(half, block), "z")
    half, across, beside = lax.optimization_barrier((half, across, beside))
    half = half.reshape(8, 4, 16, 256).transpose(1, 0, 2, 3).reshape(4, 128, 256)
    diagonal = swap(across, "core")
    other = swap(after(half, diagonal), "yh")
    out_rows = lax.all_gather(jnp.stack([half, other]), "x", axis=0)
    rows, diagonal = lax.optimization_barrier((rows, diagonal))
    xs = (own, beside, across, diagonal)

    line = ("x", "yh", "z")
    right = [(i, (i + 1) % 64) for i in range(64)]
    left = [((i + 1) % 64, i) for i in range(64)]
    first, here, queries = project(ids, gains, rows, xs)
    from_left, from_right = lax.ppermute(here, line, right), lax.ppermute(here, line, left)

    back = [(i + 1, i) for i in range(3)]
    next_level = lax.ppermute(after(levels[:1], here), ("yl", "core"), back)
    next_x = lax.ppermute(after(first_x, here), ("yl", "core"), back)
    from_left, from_right, next_x, next_level = lax.optimization_barrier(
        (from_left, from_right, next_x, next_level)
    )
    pair = jax.ShapeDtypeStruct((2, 128, 256), BF16)
    o = call(
        attend_kernel,
        [pair] * 4,
        (ids,),
        (),
        (queries, first, here, from_left, from_right),
        scratch=[pltpu.VMEM((4, 2, 128, 256), BF16)],
    )
    out_other = swap(after(out_rows, o[0]), "core")
    o = (
        o[0],
        swap(o[1], "core"),
        swap(o[2], "yl"),
        lax.ppermute(o[3], ("yl", "core"), [(i, 3 - i) for i in range(4)]),
    )

    now = jnp.concatenate([levels[1:], next_level])
    a_now = alpha_bar(now)
    a_later = alpha_bar(jnp.maximum(now - LEVELS // FRAMES, 0))
    coefs = jnp.stack(
        [jnp.sqrt(a_later), jnp.sqrt(1.0 - a_now), 1.0 / jnp.sqrt(a_now), jnp.sqrt(1.0 - a_later)],
        axis=1,
    ).reshape(8)
    return call(
        finish_kernel,
        jax.ShapeDtypeStruct(frames_in.shape, BF16),
        (ids, coefs),
        (out_rows, out_other, frames_in, next_x, fresh),
        o,
        scratch=[
            pltpu.VMEM((2, 4, 4, 2, 128, 256), BF16),
            pltpu.VMEM((3, 128, 2048), BF16),
            pltpu.VMEM((8, 256, 128), BF16),
            pltpu.SemaphoreType.DMA((2, 2)),
            pltpu.SemaphoreType.DMA((3,)),
        ],
    )


def solution(mesh):
    cut = Mesh(mesh.devices.reshape(SIZES), AXES)
    frame, space = ("yl", "core"), ("x", "yh", "z")
    return jax.shard_map(
        body,
        mesh=cut,
        in_specs=(
            P(frame, space, None),
            P(frame),
            P(space, None),
            P(),
            P(space, None),
            P(),
            P(space, None),
        ),
        out_specs=P(frame, space, None),
        check_vma=False,
    )
```

```python
import functools
import math

import jax
import jax.numpy as jnp
from jax import lax
from jax.experimental import pallas as pl
from jax.experimental.pallas import tpu as pltpu
from jax.sharding import Mesh, PartitionSpec as P

LEVELS = 1000
FRAMES = 8
F32 = jnp.float32
BF16 = jnp.bfloat16
AXES = ("yl", "core", "x", "yh", "z")
SIZES = (2, 2, 4, 2, 8)
SIZE = dict(zip(AXES, SIZES))
NEAR_LIMIT = 20 * 1024 * 1024
FAR_LIMIT = 56 * 1024 * 1024


def embed(levels, freq_count):
    half = freq_count // 2
    freqs = jnp.exp(-math.log(10000.0) * jnp.arange(half, dtype=F32) / half)
    angles = levels.astype(F32)[:, None] * freqs[None, :]
    return jnp.concatenate([jnp.cos(angles), jnp.sin(angles)], axis=1).astype(BF16)


def alpha_bar(steps):
    frac = steps.astype(F32) / LEVELS
    return jnp.cos((frac + 0.008) / 1.008 * (math.pi / 2)) ** 2


def swap(array, axis):
    return lax.ppermute(array, axis, [(0, 1), (1, 0)])


def shift(array, axis, by):
    n = SIZE[axis]
    return lax.ppermute(array, axis, [(i, (i + by) % n) for i in range(n)])


def after(array, *others):
    return lax.optimization_barrier((array, *others))[0]


def gather(array, axis):
    size = math.prod(SIZE[a] for a in ((axis,) if isinstance(axis, str) else axis))
    copies = lax.optimization_barrier(jnp.broadcast_to(array[None], (size, *array.shape)))
    return lax.all_to_all(copies, axis, 0, 0)


def call(body, out_shape, scalars, far, near=(), scratch=()):
    limit = FAR_LIMIT if far else NEAR_LIMIT
    specs = [pl.BlockSpec(memory_space=pltpu.SMEM)] * len(scalars)
    specs += [pl.BlockSpec(memory_space=pl.ANY)] * len(far)
    specs += [pl.BlockSpec(memory_space=pltpu.VMEM)] * len(near)
    return pl.pallas_call(
        body,
        out_shape=out_shape,
        in_specs=specs,
        out_specs=jax.tree.map(lambda _: pl.BlockSpec(memory_space=pltpu.VMEM), out_shape),
        scratch_shapes=list(scratch),
        compiler_params=pltpu.CompilerParams(vmem_limit_bytes=limit),
        cost_estimate=pl.CostEstimate(flops=0, bytes_accessed=0, transcendentals=0),
    )(*scalars, *far, *near)


def norm_kernel(x_ref, shift_ref, scale_ref, out_ref, copy_ref):
    copy_ref[...] = x_ref[0]
    frames, rows, width = x_ref.shape
    chunk = 32
    for f in range(frames):
        shift = shift_ref[f][None]
        scale = 1.0 + scale_ref[f][None]

        @pl.loop(0, rows // chunk)
        def _(step):
            at = pl.ds(pl.multiple_of(step * chunk, chunk), chunk)
            x = x_ref[f, at, :].astype(F32)
            mean = jnp.mean(x, axis=-1, keepdims=True)
            x = x - mean
            var = jnp.mean(x * x, axis=-1, keepdims=True)
            out_ref[f, at, :] = (x * lax.rsqrt(var + 1e-06) * scale + shift).astype(BF16)


def norm_rows(x, shift, scale):
    shapes = [jax.ShapeDtypeStruct(x.shape, BF16), jax.ShapeDtypeStruct(x.shape[1:], BF16)]
    return call(norm_kernel, shapes, (), (), (x, shift, scale))


def project_kernel(ids, gains, rows_hbm, x0, x1, x2, x3, first_ref, out_ref, q_ref, w_ref, x_ref, sems):
    copies = [(ref, x_ref.at[pl.ds(ids[4 + group], 2)]) for group, ref in enumerate((x0, x1, x2, x3))]
    copies += [(rows_hbm.at[z], w_ref.at[:, z]) for z in range(8)]
    copies = [pltpu.make_async_copy(a, b, sems.at[i]) for i, (a, b) in enumerate(copies)]
    for copy in copies:
        copy.start()
    for copy in copies:
        copy.wait()
    for part in range(3):
        weight = w_ref[:, :, 32 * part : 32 * part + 32].reshape(2048, 256)
        rows = x_ref[...].reshape(1024, 2048)
        got = jnp.dot(rows, weight, preferred_element_type=F32)
        if part != 1:
            heads = []
            for h in range(2):
                one = got[:, h * 128 : (h + 1) * 128]
                one = one * lax.rsqrt(jnp.mean(one * one, axis=-1, keepdims=True) + 1e-06)
                heads.append(one * gains[h] if part == 2 else one)
            got = jnp.concatenate(heads, axis=1)
        got = got.astype(BF16).reshape(FRAMES, 128, 256)
        if part < 2:
            first_ref[part] = got[0]
            out_ref[:, part] = got[1:]
        else:
            q_ref[...] = got


def project(ids, gains, rows, xs):
    return call(
        project_kernel,
        [
            jax.ShapeDtypeStruct((2, 128, 256), BF16),
            jax.ShapeDtypeStruct((FRAMES - 1, 2, 128, 256), BF16),
            jax.ShapeDtypeStruct((FRAMES, 128, 256), BF16),
        ],
        (ids, gains),
        (rows, *xs),
        scratch=[
            pltpu.VMEM((8, 8, 96, 256), BF16),
            pltpu.VMEM((FRAMES, 128, 2048), BF16),
            pltpu.SemaphoreType.DMA((12,)),
        ],
    )


def attend_kernel(ids, q_ref, first_ref, kv_ref, left_ref, right_ref, o0, o1, o2, o3, out_ref):
    inv = 1.0 / math.sqrt(128)
    rr = lax.broadcasted_iota(jnp.int32, (128, 128), 0)
    kk = lax.broadcasted_iota(jnp.int32, (128, 128), 1)
    in_left = kk >= rr
    in_right = kk <= rr
    nt = (((1,), (1,)), ((), ()))

    def frame(g, part, lanes):
        return (first_ref[part, :, lanes] if g == 0 else kv_ref[g - 1, part, :, lanes]).astype(F32)

    for f in range(1, FRAMES):
        for h in range(2):
            lanes = slice(h * 128, (h + 1) * 128)
            q = q_ref[f, :, lanes]
            left, mid, right = (
                lax.dot_general(q, ref[f - 1, 0, :, lanes], nt, preferred_element_type=F32) * inv
                for ref in (left_ref, kv_ref, right_ref)
            )
            left = jnp.where(in_left, left, -1e30)
            right = jnp.where(in_right, right, -1e30)
            q32 = q.astype(F32)
            earlier = [
                jnp.sum(q32 * frame(g, 0, lanes), axis=-1, keepdims=True) * inv for g in range(f)
            ]
            top = jnp.max(jnp.maximum(jnp.maximum(left, mid), right), axis=-1, keepdims=True)
            for score in earlier:
                top = jnp.maximum(top, score)
            left = jnp.where(in_left, jnp.exp(left - top), 0.0)
            mid = jnp.exp(mid - top)
            right = jnp.where(in_right, jnp.exp(right - top), 0.0)
            total = jnp.sum(left + mid + right, axis=-1, keepdims=True)
            acc = None
            for p, ref in ((left, left_ref), (mid, kv_ref), (right, right_ref)):
                term = jnp.dot(p.astype(BF16), ref[f - 1, 1, :, lanes], preferred_element_type=F32)
                acc = term if acc is None else acc + term
            for g, score in enumerate(earlier):
                p = jnp.exp(score - top)
                total += p
                acc += p.astype(BF16).astype(F32) * frame(g, 1, lanes)
            out_ref[ids[9 + (f - 1) // 2], (f - 1) % 2, :, lanes] = (acc / total).astype(BF16)
    out_ref[ids[12], 1] = jnp.zeros((128, 256), BF16)
    for which, ref in enumerate((o0, o1, o2, o3)):
        ref[...] = out_ref[which]


def finish_kernel(ids, coefs, wa_hbm, wb_hbm, x0_hbm, x1_hbm, fresh_hbm, o0, o1, o2, o3, out_ref, w_ref, x_ref, o_ref, sems, x_sems):
    c, last, yhi = ids[0], ids[8], ids[1]
    rows = [
        pltpu.make_async_copy(hbm, x_ref.at[i], x_sems.at[i])
        for i, hbm in enumerate((x0_hbm.at[1], x1_hbm, fresh_hbm))
    ]
    weights = [
        [
            pltpu.make_async_copy(hbm.at[:, side], w_ref.at[which, :, :, side], sems.at[which, side])
            for side in range(2)
        ]
        for which, hbm in enumerate((wa_hbm, wb_hbm))
    ]
    for copy in (*weights[0], *rows, *weights[1]):
        copy.start()
    for which, ref in enumerate((o0, o1, o2, o3)):
        for h in range(2):
            lanes = ref[:, :, h * 128 : (h + 1) * 128]
            o_ref[pl.ds(2 * ids[9 + which] + h, 1)] = lanes.reshape(1, 256, 128)
    o = [
        jnp.concatenate([o_ref[2 * x + yhi], o_ref[2 * x + 1 - yhi]], axis=1) for x in range(4)
    ]
    for which, part in ((which, part) for which in range(2) for part in range(4)):
        if part == 0:
            for copy in weights[which]:
                copy.wait()
        if which == 0 and part == 0:
            for copy in rows:
                copy.wait()
        start = (c if which == 0 else 1 - c) * 1024 + part * 256
        columns = pl.ds(pl.multiple_of(start, 256), 256)
        eps = None
        for x in range(4):
            weight = w_ref[which, x, part].reshape(256, 256)
            term = jnp.dot(o[x], weight, preferred_element_type=F32)
            eps = term if eps is None else eps + term
        for slot in range(2):
            x = x_ref[slot, :, columns].astype(F32)
            e = x + eps[slot * 128 : (slot + 1) * 128]
            done = coefs[4 * slot] * ((x - coefs[4 * slot + 1] * e) * coefs[4 * slot + 2])
            done = (done + coefs[4 * slot + 3] * e).astype(BF16)
            if slot == 1:
                done = jnp.where(last == 1, x_ref[2, :, columns], done)
            out_ref[slot, :, columns] = done


def body(frames_in, levels, fresh, w_mod, w_qkv, q_gain, w_out):
    width = frames_in.shape[2]
    yl, c = lax.axis_index("yl"), lax.axis_index("core")
    xi, yhi, zi = lax.axis_index("x"), lax.axis_index("yh"), lax.axis_index("z")
    me = 2 * yl + c
    near = [(me ^ k) for k in range(4)]
    ids = jnp.stack([c, yhi, zi, xi, *(2 * g for g in near), me // 3, *near]).astype(jnp.int32)
    gains = lax.dynamic_slice(q_gain, (2 * me,), (2,))

    columns = [lax.dynamic_slice(w_qkv, (0, 1024 * part + 256 * me), (32, 256)) for part in (1, 2, 0)]
    block = gather(jnp.concatenate(columns, axis=0), ("x", "yh"))
    rows = lax.all_gather(block, "z", axis=0)

    mod = jnp.dot(embed(levels, w_mod.shape[0]), w_mod, preferred_element_type=F32)
    own, first_x = norm_rows(frames_in, mod[:, :width], mod[:, width:])
    across = swap(after(own, block), "yl")
    beside = swap(own, "core")
    back = [(i + 1, i) for i in range(3)]
    next_level = lax.ppermute(after(levels[:1], block), ("yl", "core"), back)
    next_x = lax.ppermute(after(first_x, block), ("yl", "core"), back)

    half = lax.dynamic_slice(w_out, (0, 1024 * c), (16, 1024))
    half = half.reshape(16, 4, 256).transpose(1, 0, 2).reshape(64, 256)
    half = gather(after(half, block), "z")
    half, across, beside, next_x, next_level = lax.optimization_barrier(
        (half, across, beside, next_x, next_level)
    )
    half = half.reshape(8, 4, 16, 256).transpose(1, 0, 2, 3).reshape(4, 128, 256)
    diagonal = swap(across, "core")
    other = swap(after(half, diagonal), "yh")
    out_rows = lax.all_gather(jnp.stack([half, other]), "x", axis=0)
    rows, diagonal = lax.optimization_barrier((rows, diagonal))
    xs = (own, beside, across, diagonal)

    line = ("x", "yh", "z")
    right = [(i, (i + 1) % 64) for i in range(64)]
    left = [((i + 1) % 64, i) for i in range(64)]
    first, here, queries = project(ids, gains, rows, xs)
    from_left, from_right = lax.ppermute(here, line, right), lax.ppermute(here, line, left)

    pair = jax.ShapeDtypeStruct((2, 128, 256), BF16)
    o = call(
        attend_kernel,
        [pair] * 4,
        (ids,),
        (),
        (queries, first, here, from_left, from_right),
        scratch=[pltpu.VMEM((4, 2, 128, 256), BF16)],
    )
    out_other = swap(after(out_rows, o[0]), "core")
    o = (
        o[0],
        swap(o[1], "core"),
        swap(o[2], "yl"),
        lax.ppermute(o[3], ("yl", "core"), [(i, 3 - i) for i in range(4)]),
    )

    now = jnp.concatenate([levels[1:], next_level])
    a_now = alpha_bar(now)
    a_later = alpha_bar(jnp.maximum(now - LEVELS // FRAMES, 0))
    coefs = jnp.stack(
        [jnp.sqrt(a_later), jnp.sqrt(1.0 - a_now), 1.0 / jnp.sqrt(a_now), jnp.sqrt(1.0 - a_later)],
        axis=1,
    ).reshape(8)
    return call(
        finish_kernel,
        jax.ShapeDtypeStruct(frames_in.shape, BF16),
        (ids, coefs),
        (out_rows, out_other, frames_in, next_x, fresh),
        o,
        scratch=[
            pltpu.VMEM((2, 4, 4, 2, 128, 256), BF16),
            pltpu.VMEM((3, 128, 2048), BF16),
            pltpu.VMEM((8, 256, 128), BF16),
            pltpu.SemaphoreType.DMA((2, 2)),
            pltpu.SemaphoreType.DMA((3,)),
        ],
    )


def solution(mesh):
    cut = Mesh(mesh.devices.reshape(SIZES), AXES)
    frame, space = ("yl", "core"), ("x", "yh", "z")
    return jax.shard_map(
        body,
        mesh=cut,
        in_specs=(
            P(frame, space, None),
            P(frame),
            P(space, None),
            P(),
            P(space, None),
            P(),
            P(space, None),
        ),
        out_specs=P(frame, space, None),
        check_vma=False,
    )
```

```python
import functools
import math

import jax
import jax.numpy as jnp
from jax import lax
from jax.experimental import pallas as pl
from jax.experimental.pallas import tpu as pltpu
from jax.sharding import Mesh, PartitionSpec as P

LEVELS = 1000
FRAMES = 8
F32 = jnp.float32
BF16 = jnp.bfloat16
AXES = ("yl", "core", "x", "yh", "z")
SIZES = (2, 2, 4, 2, 8)
SIZE = dict(zip(AXES, SIZES))
NEAR_LIMIT = 20 * 1024 * 1024
FAR_LIMIT = 56 * 1024 * 1024


def embed(levels, freq_count):
    half = freq_count // 2
    freqs = jnp.exp(-math.log(10000.0) * jnp.arange(half, dtype=F32) / half)
    angles = levels.astype(F32)[:, None] * freqs[None, :]
    return jnp.concatenate([jnp.cos(angles), jnp.sin(angles)], axis=1).astype(BF16)


def alpha_bar(steps):
    frac = steps.astype(F32) / LEVELS
    return jnp.cos((frac + 0.008) / 1.008 * (math.pi / 2)) ** 2


def swap(array, axis):
    return lax.ppermute(array, axis, [(0, 1), (1, 0)])


def shift(array, axis, by):
    n = SIZE[axis]
    return lax.ppermute(array, axis, [(i, (i + by) % n) for i in range(n)])


def after(array, *others):
    return lax.optimization_barrier((array, *others))[0]


def gather(array, axis):
    size = math.prod(SIZE[a] for a in ((axis,) if isinstance(axis, str) else axis))
    copies = lax.optimization_barrier(jnp.broadcast_to(array[None], (size, *array.shape)))
    return lax.all_to_all(copies, axis, 0, 0)


def call(body, out_shape, scalars, far, near=(), scratch=()):
    limit = FAR_LIMIT if far else NEAR_LIMIT
    specs = [pl.BlockSpec(memory_space=pltpu.SMEM)] * len(scalars)
    specs += [pl.BlockSpec(memory_space=pl.ANY)] * len(far)
    specs += [pl.BlockSpec(memory_space=pltpu.VMEM)] * len(near)
    return pl.pallas_call(
        body,
        out_shape=out_shape,
        in_specs=specs,
        out_specs=jax.tree.map(lambda _: pl.BlockSpec(memory_space=pltpu.VMEM), out_shape),
        scratch_shapes=list(scratch),
        compiler_params=pltpu.CompilerParams(vmem_limit_bytes=limit),
        cost_estimate=pl.CostEstimate(flops=0, bytes_accessed=0, transcendentals=0),
    )(*scalars, *far, *near)


def norm_kernel(x_ref, shift_ref, scale_ref, out_ref, copy_ref):
    copy_ref[...] = x_ref[0]
    frames, rows, width = x_ref.shape
    chunk = 32
    for f in range(frames):
        shift = shift_ref[f][None]
        scale = 1.0 + scale_ref[f][None]

        @pl.loop(0, rows // chunk)
        def _(step):
            at = pl.ds(pl.multiple_of(step * chunk, chunk), chunk)
            x = x_ref[f, at, :].astype(F32)
            mean = jnp.mean(x, axis=-1, keepdims=True)
            x = x - mean
            var = jnp.mean(x * x, axis=-1, keepdims=True)
            out_ref[f, at, :] = (x * lax.rsqrt(var + 1e-06) * scale + shift).astype(BF16)


def norm_rows(x, shift, scale):
    shapes = [jax.ShapeDtypeStruct(x.shape, BF16), jax.ShapeDtypeStruct(x.shape[1:], BF16)]
    return call(norm_kernel, shapes, (), (), (x, shift, scale))


def project_kernel(ids, gains, rows_hbm, x0, x1, x2, x3, first_ref, out_ref, q_ref, w_ref, x_ref, sems):
    copies = [(ref, x_ref.at[pl.ds(ids[4 + group], 2)]) for group, ref in enumerate((x0, x1, x2, x3))]
    copies += [(rows_hbm.at[z], w_ref.at[:, z]) for z in range(8)]
    copies = [pltpu.make_async_copy(a, b, sems.at[i]) for i, (a, b) in enumerate(copies)]
    for copy in copies:
        copy.start()
    for copy in copies:
        copy.wait()
    for part in range(3):
        weight = w_ref[:, :, 32 * part : 32 * part + 32].reshape(2048, 256)
        rows = x_ref[...].reshape(1024, 2048)
        got = jnp.dot(rows, weight, preferred_element_type=F32)
        if part != 1:
            heads = []
            for h in range(2):
                one = got[:, h * 128 : (h + 1) * 128]
                one = one * lax.rsqrt(jnp.mean(one * one, axis=-1, keepdims=True) + 1e-06)
                heads.append(one * gains[h] if part == 2 else one)
            got = jnp.concatenate(heads, axis=1)
        got = got.astype(BF16).reshape(FRAMES, 128, 256)
        if part < 2:
            first_ref[part] = got[0]
            out_ref[:, part] = got[1:]
        else:
            q_ref[...] = got


def project(ids, gains, rows, xs):
    return call(
        project_kernel,
        [
            jax.ShapeDtypeStruct((2, 128, 256), BF16),
            jax.ShapeDtypeStruct((FRAMES - 1, 2, 128, 256), BF16),
            jax.ShapeDtypeStruct((FRAMES, 128, 256), BF16),
        ],
        (ids, gains),
        (rows, *xs),
        scratch=[
            pltpu.VMEM((8, 8, 96, 256), BF16),
            pltpu.VMEM((FRAMES, 128, 2048), BF16),
            pltpu.SemaphoreType.DMA((12,)),
        ],
    )


def attend_kernel(ids, q_ref, first_ref, kv_ref, left_ref, right_ref, o0, o1, o2, o3, out_ref):
    inv = 1.0 / math.sqrt(128)
    rr = lax.broadcasted_iota(jnp.int32, (128, 128), 0)
    kk = lax.broadcasted_iota(jnp.int32, (128, 128), 1)
    in_left = kk >= rr
    in_right = kk <= rr
    nt = (((1,), (1,)), ((), ()))

    def frame(g, part, lanes):
        return (first_ref[part, :, lanes] if g == 0 else kv_ref[g - 1, part, :, lanes]).astype(F32)

    for f in range(1, FRAMES):
        for h in range(2):
            lanes = slice(h * 128, (h + 1) * 128)
            q = q_ref[f, :, lanes]
            left, mid, right = (
                lax.dot_general(q, ref[f - 1, 0, :, lanes], nt, preferred_element_type=F32) * inv
                for ref in (left_ref, kv_ref, right_ref)
            )
            left = jnp.where(in_left, left, -1e30)
            right = jnp.where(in_right, right, -1e30)
            q32 = q.astype(F32)
            earlier = [
                jnp.sum(q32 * frame(g, 0, lanes), axis=-1, keepdims=True) * inv for g in range(f)
            ]
            top = jnp.max(jnp.maximum(jnp.maximum(left, mid), right), axis=-1, keepdims=True)
            for score in earlier:
                top = jnp.maximum(top, score)
            left = jnp.where(in_left, jnp.exp(left - top), 0.0)
            mid = jnp.exp(mid - top)
            right = jnp.where(in_right, jnp.exp(right - top), 0.0)
            total = jnp.sum(left + mid + right, axis=-1, keepdims=True)
            acc = None
            for p, ref in ((left, left_ref), (mid, kv_ref), (right, right_ref)):
                term = jnp.dot(p.astype(BF16), ref[f - 1, 1, :, lanes], preferred_element_type=F32)
                acc = term if acc is None else acc + term
            for g, score in enumerate(earlier):
                p = jnp.exp(score - top)
                total += p
                acc += p.astype(BF16).astype(F32) * frame(g, 1, lanes)
            out_ref[ids[9 + (f - 1) // 2], (f - 1) % 2, :, lanes] = (acc / total).astype(BF16)
    out_ref[ids[12], 1] = jnp.zeros((128, 256), BF16)
    for which, ref in enumerate((o0, o1, o2, o3)):
        ref[...] = out_ref[which]


def finish_kernel(ids, coefs, wa_hbm, wb_hbm, x0_hbm, x1_hbm, fresh_hbm, o0, o1, o2, o3, out_ref, w_ref, x_ref, o_ref, sems, x_sems):
    c, last, yhi = ids[0], ids[8], ids[1]
    rows = [
        pltpu.make_async_copy(hbm, x_ref.at[i], x_sems.at[i])
        for i, hbm in enumerate((x0_hbm.at[1], x1_hbm, fresh_hbm))
    ]
    weights = [
        [
            pltpu.make_async_copy(hbm.at[:, side], w_ref.at[which, :, :, side], sems.at[which, side])
            for side in range(2)
        ]
        for which, hbm in enumerate((wa_hbm, wb_hbm))
    ]
    for copy in (*weights[0], *rows, *weights[1]):
        copy.start()
    for which, ref in enumerate((o0, o1, o2, o3)):
        for h in range(2):
            lanes = ref[:, :, h * 128 : (h + 1) * 128]
            o_ref[pl.ds(2 * ids[9 + which] + h, 1)] = lanes.reshape(1, 256, 128)
    o = [
        jnp.concatenate([o_ref[2 * x + yhi], o_ref[2 * x + 1 - yhi]], axis=1) for x in range(4)
    ]
    for which, part in ((which, part) for which in range(2) for part in range(4)):
        if part == 0:
            for copy in weights[which]:
                copy.wait()
        if which == 0 and part == 0:
            for copy in rows:
                copy.wait()
        start = (c if which == 0 else 1 - c) * 1024 + part * 256
        columns = pl.ds(pl.multiple_of(start, 256), 256)
        eps = None
        for x in range(4):
            weight = w_ref[which, x, part].reshape(256, 256)
            term = jnp.dot(o[x], weight, preferred_element_type=F32)
            eps = term if eps is None else eps + term
        for slot in range(2):
            x = x_ref[slot, :, columns].astype(F32)
            e = x + eps[slot * 128 : (slot + 1) * 128]
            done = coefs[4 * slot] * ((x - coefs[4 * slot + 1] * e) * coefs[4 * slot + 2])
            done = (done + coefs[4 * slot + 3] * e).astype(BF16)
            if slot == 1:
                done = jnp.where(last == 1, x_ref[2, :, columns], done)
            out_ref[slot, :, columns] = done


def body(frames_in, levels, fresh, w_mod, w_qkv, q_gain, w_out):
    width = frames_in.shape[2]
    yl, c = lax.axis_index("yl"), lax.axis_index("core")
    xi, yhi, zi = lax.axis_index("x"), lax.axis_index("yh"), lax.axis_index("z")
    me = 2 * yl + c
    near = [(me ^ k) for k in range(4)]
    ids = jnp.stack([c, yhi, zi, xi, *(2 * g for g in near), me // 3, *near]).astype(jnp.int32)
    gains = lax.dynamic_slice(q_gain, (2 * me,), (2,))

    columns = [lax.dynamic_slice(w_qkv, (0, 1024 * part + 256 * me), (32, 256)) for part in (1, 2, 0)]
    block = gather(jnp.concatenate(columns, axis=0), ("x", "yh"))
    rows = lax.all_gather(block, "z", axis=0)

    mod = jnp.dot(embed(levels, w_mod.shape[0]), w_mod, preferred_element_type=F32)
    own, first_x = norm_rows(frames_in, mod[:, :width], mod[:, width:])
    across = swap(after(own, block), "yl")
    beside = swap(own, "core")
    back = [(i + 1, i) for i in range(3)]
    next_level = lax.ppermute(after(levels[:1], block), ("yl", "core"), back)
    next_x = lax.ppermute(after(first_x, block), ("yl", "core"), back)

    half = lax.dynamic_slice(w_out, (0, 1024 * c), (16, 1024))
    half = half.reshape(16, 4, 256).transpose(1, 0, 2).reshape(64, 256)
    half = gather(after(half, block), "z")
    half, across, beside, next_x, next_level = lax.optimization_barrier(
        (half, across, beside, next_x, next_level)
    )
    half = half.reshape(8, 4, 16, 256).transpose(1, 0, 2, 3).reshape(4, 128, 256)
    diagonal = swap(across, "core")
    other = swap(after(half, diagonal), "yh")
    out_rows = lax.all_gather(jnp.stack([half, other]), "x", axis=0)
    rows, diagonal = lax.optimization_barrier((rows, diagonal))
    xs = (own, beside, across, diagonal)

    line = ("x", "yh", "z")
    right = [(i, (i + 1) % 64) for i in range(64)]
    left = [((i + 1) % 64, i) for i in range(64)]
    first, here, queries = project(ids, gains, rows, xs)
    from_right = lax.ppermute(here, line, left)
    from_left = lax.ppermute(here, line, right)
    from_right, from_left = lax.optimization_barrier((from_right, from_left))

    pair = jax.ShapeDtypeStruct((2, 128, 256), BF16)
    o = call(
        attend_kernel,
        [pair] * 4,
        (ids,),
        (),
        (queries, first, here, from_left, from_right),
        scratch=[pltpu.VMEM((4, 2, 128, 256), BF16)],
    )
    out_other = swap(after(out_rows, o[0]), "core")
    o = (
        o[0],
        swap(o[1], "core"),
        swap(o[2], "yl"),
        lax.ppermute(o[3], ("yl", "core"), [(i, 3 - i) for i in range(4)]),
    )

    now = jnp.concatenate([levels[1:], next_level])
    a_now = alpha_bar(now)
    a_later = alpha_bar(jnp.maximum(now - LEVELS // FRAMES, 0))
    coefs = jnp.stack(
        [jnp.sqrt(a_later), jnp.sqrt(1.0 - a_now), 1.0 / jnp.sqrt(a_now), jnp.sqrt(1.0 - a_later)],
        axis=1,
    ).reshape(8)
    return call(
        finish_kernel,
        jax.ShapeDtypeStruct(frames_in.shape, BF16),
        (ids, coefs),
        (out_rows, out_other, frames_in, next_x, fresh),
        o,
        scratch=[
            pltpu.VMEM((2, 4, 4, 2, 128, 256), BF16),
            pltpu.VMEM((3, 128, 2048), BF16),
            pltpu.VMEM((8, 256, 128), BF16),
            pltpu.SemaphoreType.DMA((2, 2)),
            pltpu.SemaphoreType.DMA((3,)),
        ],
    )


def solution(mesh):
    cut = Mesh(mesh.devices.reshape(SIZES), AXES)
    frame, space = ("yl", "core"), ("x", "yh", "z")
    return jax.shard_map(
        body,
        mesh=cut,
        in_specs=(
            P(frame, space, None),
            P(frame),
            P(space, None),
            P(),
            P(space, None),
            P(),
            P(space, None),
        ),
        out_specs=P(frame, space, None),
        check_vma=False,
    )
```
